32 devices in a mesh: row: 4 (over z), col: 8 (over y, x, core).
Axes of the slice: x: 2, y: 2, z: 4, core: 2. Of those that a mesh axis runs over, the one named last changes fastest.
Arguments:
- stiffness: float32 [8, 4, 512, 4, 8, 512], P(None, 'row', None, None, 'col'), may hold values from -7 to 7
- lower_panel: float32 [8, 4, 512, 512], P(None, 'row'), may hold values from -0.25 to 0.25
- diag_inverse: float32 [512, 512], replicated, as said below
Outputs:
- reduced: float32 [8, 4, 512, 4, 8, 512], P(None, 'row', None, None, 'col')
The draws below stay inside these ranges and needn't reach their ends.
Inputs may be any that keep to these rules, and one draw needn't show every extreme that they name: diag_inverse is lower triangular with a positive diagonal.
All inputs are finite; a program needn't handle non-finite values.
Results may differ from the reference program's by a relative error of at most 0.000062.
Values sent between devices are 32-bit elements; how exact they have to be, the bound alone decides.
No kernel may reach another device: no remote copies, remote signals or barrier semaphores. Data moves between devices by JAX's collectives and lax.ppermute only.
A program may use at most 192 MiB of HBM per device.

```python
import jax
import jax.numpy as jnp
from jax import lax

NB = 512
ORDER = 16384
BR = 8
BC = 4
N_ROW = 4
N_COL = 8


def draw_stiffness(key, part):
    first = jax.random.fold_in(key, 0)
    base = jnp.clip(jax.random.normal(first, (ORDER, ORDER), jnp.float32), -4.0, 4.0)
    sym = 0.5 * (base + base.T)
    return sym.reshape(BR, N_ROW, NB, BC, N_COL, NB)


def draw_diag_inverse(key, part):
    first, second = jax.random.split(key)
    diag = jnp.exp(jax.random.uniform(first, (NB,), jnp.float32, -0.7, 0.7))
    off = jax.random.normal(second, (NB, NB), jnp.float32)
    off = jnp.tril(off, -1) * (0.5 / jnp.sqrt(jnp.float32(NB)))
    return off + jnp.diag(diag)


def steps_of(rng, shape, pieces, low, top_value):
    factor_of = 1.0
    for dim, parts in pieces:
        draws = jax.random.uniform(jax.random.fold_in(jax.random.fold_in(rng, 6), dim), (parts,), jnp.float32, low / len(pieces), top_value / len(pieces))
        factor_of = factor_of * jnp.repeat(jnp.exp(draws), shape[dim] // parts).reshape((-1,) + (1,) * (len(shape) - 1 - dim))
    return factor_of


def centred(rng, extent, spread, limit, cuts=(), held_as=jnp.bfloat16):
    gain = steps_of(rng, extent, cuts, -0.22, 0.18) if cuts else 1.0
    values = jax.random.normal(rng, extent, jnp.float32) * spread * gain
    return jnp.minimum(jnp.maximum(values, -limit), limit).astype(held_as)


def setup_inputs(seed: int = 0) -> dict:
    key_list = jax.random.split(jax.random.key(seed), 4)
    return {
        "stiffness": draw_stiffness(jax.random.fold_in(key_list[3], 71), 0),
        "lower_panel": centred(key_list[1], (BR, N_ROW, NB, NB), NB ** -0.5, 0.25, ((1, 4),), jnp.float32),
        "diag_inverse": draw_diag_inverse(jax.random.fold_in(key_list[3], 71), 0),
    }


def reference(stiffness, lower_panel, diag_inverse):
    highest = lax.Precision.HIGHEST
    shape = stiffness.shape
    whole = stiffness.reshape(ORDER, ORDER)
    lower = lower_panel.reshape(ORDER, NB)
    lower = lower.at[:NB, :].set(jnp.zeros((NB, NB), jnp.float32))
    corner = whole[:NB, :NB]
    c_block = jnp.dot(jnp.dot(diag_inverse, corner, precision=highest), diag_inverse.T, precision=highest)
    panel = whole[:, :NB].at[:NB, :].set(jnp.zeros((NB, NB), jnp.float32))
    lower_c = jnp.dot(lower, c_block, precision=highest)
    w_panel = jnp.dot(panel, diag_inverse.T, precision=highest) - 0.5 * lower_c
    update = whole - jnp.dot(w_panel, lower.T, precision=highest) - jnp.dot(lower, w_panel.T, precision=highest)
    final_panel = w_panel - 0.5 * lower_c
    update = update.at[:, :NB].set(final_panel)
    update = update.at[:NB, :].set(final_panel.T)
    update = update.at[:NB, :NB].set(c_block)
    return update.reshape(shape)
```

```python
import functools

import jax
import jax.numpy as jnp
from jax import lax
from jax.experimental import pallas as pl
from jax.experimental.pallas import tpu as pltpu
from jax.sharding import PartitionSpec as P

LANES = 128
F32, BF16 = jnp.float32, jnp.bfloat16


def halves(x):
    high = x.astype(BF16)
    return high, (x - high.astype(F32)).astype(BF16)


def dot3(a, b, contract):
    dims = (contract, ((), ()))
    mul = functools.partial(lax.dot_general, dimension_numbers=dims, preferred_element_type=F32)
    return mul(a[0], b[0]) + (mul(a[1], b[0]) + mul(a[0], b[1]))


def factor_kernel(parts, flag, s_ref, d_ref, *refs):
    lows, tops = refs[:parts], refs[parts : 2 * parts]
    high_ref, low_ref = refs[2 * parts :]
    nb = d_ref.shape[0]
    piece = nb // parts
    per = nb // LANES

    @pl.when(flag[0] == 0)
    def _():
        s = halves(s_ref[...])
        d = halves(d_ref[...])
        add = None
        for h in range(parts):
            flat = tops[h]
            top = jnp.concatenate([flat[pl.ds(q, piece, stride=per), :] for q in range(per)], axis=1)
            span = slice(h * piece, (h + 1) * piece)
            part = dot3((d[0][:, span], d[1][:, span]), halves(top), ((1,), (0,)))
            add = part if add is None else add + part
        for h in range(parts):
            span = slice(h * piece, (h + 1) * piece)
            out = dot3(s, halves(lows[h][...]), ((1,), (1,)))
            high_ref[:nb, span], low_ref[:nb, span] = halves(out[:nb])
            high_ref[nb:, span], low_ref[nb:, span] = halves(add[:, span] - out[nb:])

    @pl.when(flag[0] != 0)
    def _():
        high_ref[:nb], low_ref[:nb] = halves(-s_ref[:nb])
        high_ref[nb:], low_ref[nb:] = halves(s_ref[nb:])


def factors(flag, s, d, lows, tops):
    nb = d.shape[0]
    parts = len(lows)
    vmem = pl.BlockSpec(memory_space=pltpu.VMEM)
    return pl.pallas_call(
        functools.partial(factor_kernel, parts),
        out_shape=[jax.ShapeDtypeStruct((2 * nb, nb), BF16)] * 2,
        in_specs=[pl.BlockSpec(memory_space=pltpu.SMEM)] + [vmem] * (2 + 2 * parts),
        out_specs=[vmem] * 2,
        compiler_params=pltpu.CompilerParams(vmem_limit_bytes=40 << 20),
        cost_estimate=pl.CostEstimate(flops=18 * nb**3, bytes_accessed=24 * nb * nb, transcendentals=0),
        name="factors",
    )(flag, s, d, *lows, *tops)


def split_kernel(per, flags, panel_ref, high_ref, low_ref):
    tile = high_ref.shape[0]
    drop = jnp.logical_and(flags[0] != 0, pl.program_id(0) == 0)
    for q in range(per):
        value = jnp.where(drop, 0.0, panel_ref[pl.ds(q, tile, stride=per), :])
        span = slice(q * LANES, (q + 1) * LANES)
        high_ref[:, span], low_ref[:, span] = halves(value)


def split_panel(flags, panel, tile, per):
    rows = panel.shape[0] // per
    out = pl.BlockSpec((tile, per * LANES), lambda i: (i, 0))
    return pl.pallas_call(
        functools.partial(split_kernel, per),
        grid=(rows // tile,),
        out_shape=[jax.ShapeDtypeStruct((rows, per * LANES), BF16)] * 2,
        in_specs=[pl.BlockSpec(memory_space=pltpu.SMEM), pl.BlockSpec((tile * per, LANES), lambda i: (i, 0))],
        out_specs=[out] * 2,
        compiler_params=pltpu.CompilerParams(vmem_limit_bytes=40 << 20),
        cost_estimate=pl.CostEstimate(flops=0, bytes_accessed=8 * rows * per * LANES, transcendentals=0),
        name="split_panel",
    )(flags, panel)


def split_lower_kernel(flags, lower_ref, high_ref, low_ref):
    top = jnp.logical_and(flags[0] != 0, pl.program_id(0) == 0)
    shape = lower_ref.shape
    same = lax.broadcasted_iota(jnp.int32, shape, 0) == lax.broadcasted_iota(jnp.int32, shape, 1)
    value = jnp.where(top, jnp.where(same, -1.0, 0.0), lower_ref[...])
    high_ref[...], low_ref[...] = halves(value)


def split_lower(flags, lower, tile):
    spec = pl.BlockSpec((tile, lower.shape[1]), lambda i: (i, 0))
    return pl.pallas_call(
        split_lower_kernel,
        grid=(lower.shape[0] // tile,),
        out_shape=[jax.ShapeDtypeStruct(lower.shape, BF16)] * 2,
        in_specs=[pl.BlockSpec(memory_space=pltpu.SMEM), spec],
        out_specs=[spec] * 2,
        compiler_params=pltpu.CompilerParams(vmem_limit_bytes=40 << 20),
        cost_estimate=pl.CostEstimate(flops=0, bytes_accessed=8 * lower.size, transcendentals=0),
        name="split_lower",
    )(flags, lower)


def update_kernel(group, start, flags, a_ref, ph_ref, pl_ref, lh_ref, ll_ref, *refs):
    out_ref, token_ref = refs[-2:]
    token_ref[...] = jnp.zeros_like(token_ref)
    tile = a_ref.shape[0]
    chunks = a_ref.shape[1]
    depth = ph_ref.shape[1]
    per = refs[0].shape[1] // LANES
    a2 = a_ref.reshape(tile * chunks, LANES)
    o2 = out_ref.reshape(tile * chunks, LANES)
    top = jnp.logical_and(flags[0] != 0, pl.program_id(0) == -start)
    first = jnp.logical_and(flags[1] != 0, group == 0)
    mul = functools.partial(jnp.dot, preferred_element_type=F32)
    for pair in range(chunks // 2):
        block, at = divmod(2 * pair, per)
        yh_ref, yl_ref = refs[2 * block], refs[2 * block + 1]
        span = slice(at * LANES, (at + 2) * LANES)
        acc = mul(ph_ref[...], yh_ref[:depth, span])
        acc = acc + mul(pl_ref[...], yh_ref[:depth, span])
        acc = acc + mul(ph_ref[...], yl_ref[:depth, span])
        acc = acc + mul(lh_ref[...], yh_ref[depth:, span])
        acc = acc + mul(ll_ref[...], yh_ref[depth:, span])
        acc = acc + mul(lh_ref[...], yl_ref[depth:, span])
        drop = jnp.logical_or(top, first) if block == 0 else top
        for k in range(2):
            where = (pl.ds(2 * pair + k, tile, stride=chunks), slice(None))
            a = jnp.where(drop, 0.0, a2[where])
            o2[where] = a - acc[:, k * LANES : (k + 1) * LANES]


def update(group, start, steps, flags, a, xs, ys, previous, tile):
    rows, chunks, _ = a.shape
    depth = xs[0].shape[1]
    nb = ys[0].shape[1]
    mine = len(ys) // 2 * (nb // LANES)
    spec = pl.BlockSpec((tile, mine, LANES), lambda i: (i + start, group, 0))
    xspec = pl.BlockSpec((tile, depth), lambda i: (i + start, 0))
    yspec = pl.BlockSpec((2 * depth, nb), lambda i: (0, 0))
    operands = [flags, a, *xs, *ys]
    in_specs = [pl.BlockSpec(memory_space=pltpu.SMEM), spec] + [xspec] * len(xs) + [yspec] * len(ys)
    aliases = {}
    if previous is not None:
        aliases = {len(operands): 0}
        operands.append(previous)
        in_specs.append(pl.BlockSpec(memory_space=pl.ANY))
    done = steps * tile
    return pl.pallas_call(
        functools.partial(update_kernel, group, start),
        grid=(steps,),
        out_shape=[jax.ShapeDtypeStruct(a.shape, F32), jax.ShapeDtypeStruct((8, LANES), F32)],
        in_specs=in_specs,
        out_specs=[spec, pl.BlockSpec((8, LANES), lambda i: (0, 0))],
        input_output_aliases=aliases,
        compiler_params=pltpu.CompilerParams(vmem_limit_bytes=56 << 20),
        cost_estimate=pl.CostEstimate(
            flops=12 * done * mine * LANES * depth, bytes_accessed=8 * done * mine * LANES + 8 * done * depth,
            transcendentals=0,
        ),
        name="update",
    )(*operands)


def tie(sent, *waits):
    return list(lax.optimization_barrier((tuple(sent), waits))[0])


def arrived(got, k, distance, farthest, value):
    for d in range(1, farthest + 1):
        value = jnp.where(distance == d, got[k + d - 1], value)
    return value


def body(stiffness, lower_panel, diag_inverse):
    highest = lax.Precision.HIGHEST
    rows = lax.axis_size("row")
    cols = lax.axis_size("col")
    my_row = lax.axis_index("row")
    my_col = lax.axis_index("col")
    brows, _, nb, bcols, _, _ = stiffness.shape
    per = nb // LANES
    ratio = cols // rows
    split = 2
    piece = nb // split
    last = rows - 1
    home = my_col % rows
    col0 = my_col == 0
    flags = jnp.stack([my_row == 0, col0]).astype(jnp.int32)

    def dev(r, c):
        return r * cols + c

    def send(x, pairs):
        return lax.ppermute(x, ("row", "col"), pairs)

    a4 = stiffness.reshape(brows * nb, bcols, per, LANES)
    a = stiffness.reshape(brows * nb, bcols * per, LANES)
    lower = lower_panel[:, 0]

    top_own = [a4[s * piece : (s + 1) * piece, b].reshape(-1, LANES) for b in range(bcols) for s in range(split)]
    top_pairs = [(dev(r, c), dev(r + 1, c)) for r in range(last) for c in range(cols)]
    grouped = lower.reshape(bcols, ratio, nb, nb)
    mine = lax.dynamic_index_in_dim(grouped, my_col // rows, 1, keepdims=False)
    up_own = [mine[b, s * piece : (s + 1) * piece] for b in range(bcols) for s in range(split)]
    down_own = [mine[b] for b in range(bcols)]
    detour = {c: c ^ 2 for c in range(cols) if c % rows == 1} if (rows, cols) == (4, 8) else {}
    starts = {c: c % rows for c in range(cols) if c not in detour}
    starts.update({via: c % rows for c, via in detour.items()})
    up_pairs = [(dev(r, c), dev(r + 1, c)) for c, s in starts.items() for r in range(s, last)]
    up_source = my_row == home
    if detour:
        up_source = jnp.where(home == 3, my_row == 1, up_source)
    down_pairs = [(dev(r, c), dev(r - 1, c)) for c in range(cols) for r in range(c % rows, 0, -1)]
    side_pairs = [(dev(r, via), dev(r, c)) for c, via in detour.items() for r in range(2, rows)]

    panel = a4[:, 0].reshape(-1, LANES)
    share = panel.shape[0] // cols

    def nxt(own, got, source):
        t = len(got)
        if t == 0:
            return own[0]
        return jnp.where(source, own[t], got[-1]) if t < len(own) else got[-1]

    def top_at(k):
        return arrived(top_got, k, my_row, last, top_own[k])

    def low_at(k):
        value = arrived(up_got, k, my_row - home, last, up_own[k])
        down_k = [g[(k % split) * piece : (k % split + 1) * piece] for g in down_got]
        value = arrived(down_k, k // split, home - my_row, last, value)
        for r in range(2, rows) if detour else ():
            here = jnp.logical_and(home == 1, my_row == r)
            value = jnp.where(here, side_got[k + r - 2], value)
        return value

    def factors_of(b):
        special = jnp.logical_and(col0, b == 0).astype(jnp.int32).reshape(1)
        here = range(b * split, (b + 1) * split)
        return factors(special, s, diag_inverse, [low_at(k) for k in here], [top_at(k) for k in here])

    def spread(x, bit):
        span = 1 << bit
        pairs = [(dev(r, c), dev(r, c + span)) for r in range(rows) for c in range(0, cols, 2 * span)]
        return jnp.where(my_col % (2 * span) == span, send(x, pairs), x)

    def scales():
        c_block = jnp.dot(diag_inverse, corner.reshape(nb, nb), precision=highest)
        c_block = jnp.dot(c_block, diag_inverse.T, precision=highest)
        return jnp.concatenate([diag_inverse.T, c_block])

    count = bcols * split
    top_steps = count + last - 1
    down_steps = bcols + last - 1
    corner_at = split + last - 1
    bits = cols.bit_length() - 1
    ready = 2 * split + last - 1
    parts = max(top_steps - ready - 1, 1)
    early = bcols > 2 and corner_at + bits <= ready + 1 and top_steps - ready > 1
    bit = bits
    bounds = [brows * k // parts for k in range(parts + 1)]
    top_got, up_got, down_got, side_got = [], [], [], []
    corner = panel_all = out = s = None
    ys, waits = {}, []
    for t in range(top_steps):
        sent = [nxt(top_own, top_got, my_row == 0)]
        if t == corner_at:
            corner = jnp.concatenate([top_at(k) for k in range(split)])
        hop = t >= corner_at and bit > 0
        if hop:
            bit -= 1
            sent.append(corner)
        if t:
            tied = [top_got[-1], *waits]
            tied += up_got[t - 1 :] if t >= ready else up_got[t - 2 : t - 1]
            sent = tie(sent, *tied)
        top_got.append(send(sent[0], top_pairs))
        if hop:
            corner = spread(sent[1], bit)
        sent = [nxt(up_own, up_got, up_source)]
        if detour and t:
            sent.append(up_got[t - 1])
        go_down = len(down_got) < down_steps and t >= (4 * len(down_got) + 1) // 3
        if go_down:
            sent.append(nxt(down_own, down_got, my_row == home))
        if t:
            sent = tie(sent, up_got[-1], top_got[t - 1], *waits)
        up_got.append(send(sent[0], up_pairs))
        if detour and t:
            side_got.append(send(sent[1], side_pairs))
        if go_down:
            down_got.append(send(sent[-1], down_pairs))
        waits = []
        if t == 0:
            deals = [panel[c * share : (c + 1) * share] for c in range(cols)]
            dealt = [send(deals[c], [(dev(r, 0), dev(r, c)) for r in range(rows)]) for c in range(1, cols)]
        if t == 1:
            share_got = jnp.where(col0, deals[0], functools.reduce(jnp.add, dealt))
            (share_got,) = tie([share_got], top_got[1], up_got[1])
            panel_all = lax.all_gather(share_got, "col", axis=0, tiled=True)
            right = split_lower(flags, lower.reshape(brows * nb, nb), nb)
            waits = [right[0]]
        if early and t == ready:
            s = scales()
            xs = [*split_panel(flags, panel_all, nb, per), *right]
            ys[0] = [*factors_of(0), *factors_of(1)]
            waits = [xs[0], ys[0][0], ys[0][2]]
        if early and t > ready:
            k = t - ready - 1
            out, token = update(
                0, bounds[k], bounds[k + 1] - bounds[k], flags, a, xs, ys[0], out, nb
            )
            waits = [token]
    if detour:
        side_got.append(send(up_got[-1], side_pairs))
    while len(down_got) < down_steps:
        down_got.append(send(nxt(down_own, down_got, my_row == home), down_pairs))
    if not early:
        while bit > 0:
            bit -= 1
            corner = spread(corner, bit)
        s = scales()
        xs = [*split_panel(flags, panel_all, nb, per), *right]
    for group in range(int(early), bcols // 2):
        ys[group] = [*factors_of(2 * group), *factors_of(2 * group + 1)]
        out, _ = update(group, 0, brows, flags, a, xs, ys[group], out, nb)
    return out.reshape(stiffness.shape)


def solution(mesh):
    in_specs = (P(None, "row", None, None, "col", None), P(None, "row", None, None), P())
    out_specs = P(None, "row", None, None, "col", None)
    return jax.shard_map(body, mesh=mesh, in_specs=in_specs, out_specs=out_specs, check_vma=False)
```

```python
import functools

import jax
import jax.numpy as jnp
from jax import lax
from jax.experimental import pallas as pl
from jax.experimental.pallas import tpu as pltpu
from jax.sharding import PartitionSpec as P

LANES = 128
F32, BF16 = jnp.float32, jnp.bfloat16


def halves(x):
    high = x.astype(BF16)
    return high, (x - high.astype(F32)).astype(BF16)


def dot3(a, b, contract):
    dims = (contract, ((), ()))
    mul = functools.partial(lax.dot_general, dimension_numbers=dims, preferred_element_type=F32)
    return mul(a[0], b[0]) + (mul(a[1], b[0]) + mul(a[0], b[1]))


def factor_kernel(parts, flag, s_ref, d_ref, *refs):
    lows, tops = refs[:parts], refs[parts : 2 * parts]
    high_ref, low_ref = refs[2 * parts :]
    nb = d_ref.shape[0]
    piece = nb // parts
    per = nb // LANES

    @pl.when(flag[0] == 0)
    def _():
        s = halves(s_ref[...])
        d = halves(d_ref[...])
        add = None
        for h in range(parts):
            flat = tops[h]
            top = jnp.concatenate([flat[pl.ds(q, piece, stride=per), :] for q in range(per)], axis=1)
            span = slice(h * piece, (h + 1) * piece)
            part = dot3((d[0][:, span], d[1][:, span]), halves(top), ((1,), (0,)))
            add = part if add is None else add + part
        for h in range(parts):
            span = slice(h * piece, (h + 1) * piece)
            out = dot3(s, halves(lows[h][...]), ((1,), (1,)))
            high_ref[:nb, span], low_ref[:nb, span] = halves(out[:nb])
            high_ref[nb:, span], low_ref[nb:, span] = halves(add[:, span] - out[nb:])

    @pl.when(flag[0] != 0)
    def _():
        high_ref[:nb], low_ref[:nb] = halves(-s_ref[:nb])
        high_ref[nb:], low_ref[nb:] = halves(s_ref[nb:])


def factors(flag, s, d, lows, tops):
    nb = d.shape[0]
    parts = len(lows)
    vmem = pl.BlockSpec(memory_space=pltpu.VMEM)
    return pl.pallas_call(
        functools.partial(factor_kernel, parts),
        out_shape=[jax.ShapeDtypeStruct((2 * nb, nb), BF16)] * 2,
        in_specs=[pl.BlockSpec(memory_space=pltpu.SMEM)] + [vmem] * (2 + 2 * parts),
        out_specs=[vmem] * 2,
        compiler_params=pltpu.CompilerParams(vmem_limit_bytes=40 << 20),
        cost_estimate=pl.CostEstimate(flops=18 * nb**3, bytes_accessed=24 * nb * nb, transcendentals=0),
        name="factors",
    )(flag, s, d, *lows, *tops)


def split_kernel(per, flags, panel_ref, high_ref, low_ref):
    tile = high_ref.shape[0]
    drop = jnp.logical_and(flags[0] != 0, pl.program_id(0) == 0)
    for q in range(per):
        value = jnp.where(drop, 0.0, panel_ref[pl.ds(q, tile, stride=per), :])
        span = slice(q * LANES, (q + 1) * LANES)
        high_ref[:, span], low_ref[:, span] = halves(value)


def split_panel(flags, panel, tile, per):
    rows = panel.shape[0] // per
    out = pl.BlockSpec((tile, per * LANES), lambda i: (i, 0))
    return pl.pallas_call(
        functools.partial(split_kernel, per),
        grid=(rows // tile,),
        out_shape=[jax.ShapeDtypeStruct((rows, per * LANES), BF16)] * 2,
        in_specs=[pl.BlockSpec(memory_space=pltpu.SMEM), pl.BlockSpec((tile * per, LANES), lambda i: (i, 0))],
        out_specs=[out] * 2,
        compiler_params=pltpu.CompilerParams(vmem_limit_bytes=40 << 20),
        cost_estimate=pl.CostEstimate(flops=0, bytes_accessed=8 * rows * per * LANES, transcendentals=0),
        name="split_panel",
    )(flags, panel)


def split_lower_kernel(flags, lower_ref, high_ref, low_ref):
    top = jnp.logical_and(flags[0] != 0, pl.program_id(0) == 0)
    shape = lower_ref.shape
    same = lax.broadcasted_iota(jnp.int32, shape, 0) == lax.broadcasted_iota(jnp.int32, shape, 1)
    value = jnp.where(top, jnp.where(same, -1.0, 0.0), lower_ref[...])
    high_ref[...], low_ref[...] = halves(value)


def split_lower(flags, lower, tile):
    spec = pl.BlockSpec((tile, lower.shape[1]), lambda i: (i, 0))
    return pl.pallas_call(
        split_lower_kernel,
        grid=(lower.shape[0] // tile,),
        out_shape=[jax.ShapeDtypeStruct(lower.shape, BF16)] * 2,
        in_specs=[pl.BlockSpec(memory_space=pltpu.SMEM), spec],
        out_specs=[spec] * 2,
        compiler_params=pltpu.CompilerParams(vmem_limit_bytes=40 << 20),
        cost_estimate=pl.CostEstimate(flops=0, bytes_accessed=8 * lower.size, transcendentals=0),
        name="split_lower",
    )(flags, lower)


def update_kernel(group, start, flags, a_ref, ph_ref, pl_ref, lh_ref, ll_ref, *refs):
    out_ref, token_ref = refs[-2:]
    token_ref[...] = jnp.zeros_like(token_ref)
    tile = a_ref.shape[0]
    chunks = a_ref.shape[1]
    depth = ph_ref.shape[1]
    per = refs[0].shape[1] // LANES
    a2 = a_ref.reshape(tile * chunks, LANES)
    o2 = out_ref.reshape(tile * chunks, LANES)
    top = jnp.logical_and(flags[0] != 0, pl.program_id(0) == -start)
    first = jnp.logical_and(flags[1] != 0, group == 0)
    mul = functools.partial(jnp.dot, preferred_element_type=F32)
    for pair in range(chunks // 2):
        block, at = divmod(2 * pair, per)
        yh_ref, yl_ref = refs[2 * block], refs[2 * block + 1]
        span = slice(at * LANES, (at + 2) * LANES)
        acc = mul(ph_ref[...], yh_ref[:depth, span])
        acc = acc + mul(pl_ref[...], yh_ref[:depth, span])
        acc = acc + mul(ph_ref[...], yl_ref[:depth, span])
        acc = acc + mul(lh_ref[...], yh_ref[depth:, span])
        acc = acc + mul(ll_ref[...], yh_ref[depth:, span])
        acc = acc + mul(lh_ref[...], yl_ref[depth:, span])
        drop = jnp.logical_or(top, first) if block == 0 else top
        for k in range(2):
            where = (pl.ds(2 * pair + k, tile, stride=chunks), slice(None))
            a = jnp.where(drop, 0.0, a2[where])
            o2[where] = a - acc[:, k * LANES : (k + 1) * LANES]


def update(group, start, steps, flags, a, xs, ys, previous, tile):
    rows, chunks, _ = a.shape
    depth = xs[0].shape[1]
    nb = ys[0].shape[1]
    mine = len(ys) // 2 * (nb // LANES)
    spec = pl.BlockSpec((tile, mine, LANES), lambda i: (i + start, group, 0))
    xspec = pl.BlockSpec((tile, depth), lambda i: (i + start, 0))
    yspec = pl.BlockSpec((2 * depth, nb), lambda i: (0, 0))
    operands = [flags, a, *xs, *ys]
    in_specs = [pl.BlockSpec(memory_space=pltpu.SMEM), spec] + [xspec] * len(xs) + [yspec] * len(ys)
    aliases = {}
    if previous is not None:
        aliases = {len(operands): 0}
        operands.append(previous)
        in_specs.append(pl.BlockSpec(memory_space=pl.ANY))
    done = steps * tile
    return pl.pallas_call(
        functools.partial(update_kernel, group, start),
        grid=(steps,),
        out_shape=[jax.ShapeDtypeStruct(a.shape, F32), jax.ShapeDtypeStruct((8, LANES), F32)],
        in_specs=in_specs,
        out_specs=[spec, pl.BlockSpec((8, LANES), lambda i: (0, 0))],
        input_output_aliases=aliases,
        compiler_params=pltpu.CompilerParams(vmem_limit_bytes=56 << 20),
        cost_estimate=pl.CostEstimate(
            flops=12 * done * mine * LANES * depth, bytes_accessed=8 * done * mine * LANES + 8 * done * depth,
            transcendentals=0,
        ),
        name="update",
    )(*operands)


def tie(sent, *waits):
    return list(lax.optimization_barrier((tuple(sent), waits))[0])


def arrived(got, k, distance, farthest, value):
    for d in range(1, farthest + 1):
        value = jnp.where(distance == d, got[k + d - 1], value)
    return value


def body(stiffness, lower_panel, diag_inverse):
    highest = lax.Precision.HIGHEST
    rows = lax.axis_size("row")
    cols = lax.axis_size("col")
    my_row = lax.axis_index("row")
    my_col = lax.axis_index("col")
    brows, _, nb, bcols, _, _ = stiffness.shape
    per = nb // LANES
    ratio = cols // rows
    split = 2
    piece = nb // split
    last = rows - 1
    home = my_col % rows
    col0 = my_col == 0
    flags = jnp.stack([my_row == 0, col0]).astype(jnp.int32)

    def dev(r, c):
        return r * cols + c

    def send(x, pairs):
        return lax.ppermute(x, ("row", "col"), pairs)

    a4 = stiffness.reshape(brows * nb, bcols, per, LANES)
    a = stiffness.reshape(brows * nb, bcols * per, LANES)
    lower = lower_panel[:, 0]

    top_own = [a4[s * piece : (s + 1) * piece, b].reshape(-1, LANES) for b in range(bcols) for s in range(split)]
    top_pairs = [(dev(r, c), dev(r + 1, c)) for r in range(last) for c in range(cols)]
    grouped = lower.reshape(bcols, ratio, nb, nb)
    mine = lax.dynamic_index_in_dim(grouped, my_col // rows, 1, keepdims=False)
    up_own = [mine[b, s * piece : (s + 1) * piece] for b in range(bcols) for s in range(split)]
    down_own = [mine[b] for b in range(bcols)]
    detour = {}
    starts = {c: c % rows for c in range(cols) if c not in detour}
    starts.update({via: c % rows for c, via in detour.items()})
    up_pairs = [(dev(r, c), dev(r + 1, c)) for c, s in starts.items() for r in range(s, last)]
    up_source = my_row == home
    if detour:
        up_source = jnp.where(home == 3, my_row == 1, up_source)
    down_pairs = [(dev(r, c), dev(r - 1, c)) for c in range(cols) for r in range(c % rows, 0, -1)]
    side_pairs = [(dev(r, via), dev(r, c)) for c, via in detour.items() for r in range(2, rows)]

    panel = a4[:, 0].reshape(-1, LANES)
    share = panel.shape[0] // cols

    def nxt(own, got, source):
        t = len(got)
        if t == 0:
            return own[0]
        return jnp.where(source, own[t], got[-1]) if t < len(own) else got[-1]

    def top_at(k):
        return arrived(top_got, k, my_row, last, top_own[k])

    def low_at(k):
        value = arrived(up_got, k, my_row - home, last, up_own[k])
        down_k = [g[(k % split) * piece : (k % split + 1) * piece] for g in down_got]
        value = arrived(down_k, k // split, home - my_row, last, value)
        for r in range(2, rows) if detour else ():
            here = jnp.logical_and(home == 1, my_row == r)
            value = jnp.where(here, side_got[k + r - 2], value)
        return value

    def factors_of(b, d=diag_inverse):
        special = jnp.logical_and(col0, b == 0).astype(jnp.int32).reshape(1)
        here = range(b * split, (b + 1) * split)
        return factors(special, s, d, [low_at(k) for k in here], [top_at(k) for k in here])

    def spread(x, bit):
        span = 1 << bit
        pairs = [(dev(r, c), dev(r, c + span)) for r in range(rows) for c in range(0, cols, 2 * span)]
        return jnp.where(my_col % (2 * span) == span, send(x, pairs), x)

    def scales():
        c_block = jnp.dot(diag_inverse, corner.reshape(nb, nb), precision=highest)
        c_block = jnp.dot(c_block, diag_inverse.T, precision=highest)
        return jnp.concatenate([diag_inverse.T, c_block])

    count = bcols * split
    top_steps = count + last - 1
    down_steps = bcols + last - 1
    corner_at = split + last - 1
    bits = cols.bit_length() - 1
    ready = 2 * split + last - 1
    parts = max(top_steps - ready - 1, 1)
    early = bcols > 2 and corner_at + bits <= ready + 1 and top_steps - ready > 1
    bit = bits
    bounds = [brows * k // parts for k in range(parts + 1)]
    top_got, up_got, down_got, side_got = [], [], [], []
    corner = panel_all = out = s = None
    ys, waits = {}, []
    for t in range(top_steps):
        sent = [nxt(top_own, top_got, my_row == 0)]
        if t == corner_at:
            corner = jnp.concatenate([top_at(k) for k in range(split)])
        hop = t >= corner_at and bit > 0
        if hop:
            bit -= 1
            sent.append(corner)
        if t:
            tied = [top_got[-1], *waits]
            tied += up_got[t - 1 :] if t >= ready else up_got[t - 2 : t - 1]
            sent = tie(sent, *tied)
        top_got.append(send(sent[0], top_pairs))
        if hop:
            corner = spread(sent[1], bit)
        sent = [nxt(up_own, up_got, up_source)]
        if detour and t:
            sent.append(up_got[t - 1])
        go_down = len(down_got) < down_steps and t >= (4 * len(down_got) + 1) // 3
        if go_down:
            sent.append(nxt(down_own, down_got, my_row == home))
        if t:
            late = down_got[max(len(down_got) - 2, 0) : len(down_got) - 1] + side_got[max(t - 3, 0) : t - 2]
            sent = tie(sent, up_got[-1], top_got[t - 1], *late, *waits)
        up_got.append(send(sent[0], up_pairs))
        if detour and t:
            side_got.append(send(sent[1], side_pairs))
        if go_down:
            down_got.append(send(sent[-1], down_pairs))
        waits = []
        if t == 0:
            deals = [panel[c * share : (c + 1) * share] for c in range(cols)]
            mine_share, *deals = tie(deals, top_got[0])
            dealt = [send(x, [(dev(r, 0), dev(r, c + 1)) for r in range(rows)]) for c, x in enumerate(deals)]
        if t == 1:
            right = split_lower(flags, lower.reshape(brows * nb, nb), nb)
            waits = [right[0]]
        if t == min(3, top_steps - 1):
            share_got = jnp.where(col0, mine_share, functools.reduce(jnp.add, tie(dealt, top_got[t], up_got[t])))
            panel_all = lax.all_gather(share_got, "col", axis=0, tiled=True)
        if early and t == ready:
            s = scales()
            (own_flags,) = tie([flags], top_got[t - 1])
            xs = [*split_panel(own_flags, panel_all, nb, per), *right]
            ys[0] = [*factors_of(0)]
            waits = [xs[0], ys[0][0]]
        if early and t > ready:
            k = t - ready - 1
            own_flags, d = tie([flags, diag_inverse], top_got[t - 1], up_got[t - 1])
            if k == 0:
                ys[0] += factors_of(1, d)
            out, token = update(
                0, bounds[k], bounds[k + 1] - bounds[k], own_flags, a, xs, ys[0], out, nb
            )
            waits = [token]
            if t == top_steps - 1:
                ys[1] = [*factors_of(2, d)]
    if detour:
        side_got.append(send(up_got[-1], side_pairs))
    while len(down_got) < down_steps:
        down_got.append(send(nxt(down_own, down_got, my_row == home), down_pairs))
    if not early:
        while bit > 0:
            bit -= 1
            corner = spread(corner, bit)
        s = scales()
        xs = [*split_panel(flags, panel_all, nb, per), *right]
    for group in range(int(early), bcols // 2):
        done = ys.get(group) or factors_of(2 * group)
        ys[group] = [*done, *factors_of(2 * group + 1)]
        out, _ = update(group, 0, brows, flags, a, xs, ys[group], out, nb)
    return out.reshape(stiffness.shape)


def solution(mesh):
    in_specs = (P(None, "row", None, None, "col", None), P(None, "row", None, None), P())
    out_specs = P(None, "row", None, None, "col", None)
    return jax.shard_map(body, mesh=mesh, in_specs=in_specs, out_specs=out_specs, check_vma=False)
```

```python
import functools

import jax
import jax.numpy as jnp
from jax import lax
from jax.experimental import pallas as pl
from jax.experimental.pallas import tpu as pltpu
from jax.sharding import PartitionSpec as P

LANES = 128
F32, BF16 = jnp.float32, jnp.bfloat16


def halves(x):
    high = x.astype(BF16)
    return high, (x - high.astype(F32)).astype(BF16)


def dot3(a, b, contract):
    dims = (contract, ((), ()))
    mul = functools.partial(lax.dot_general, dimension_numbers=dims, preferred_element_type=F32)
    return mul(a[0], b[0]) + (mul(a[1], b[0]) + mul(a[0], b[1]))


def factor_kernel(parts, flag, s_ref, d_ref, *refs):
    lows, tops = refs[:parts], refs[parts : 2 * parts]
    high_ref, low_ref = refs[2 * parts :]
    nb = d_ref.shape[0]
    piece = nb // parts
    per = nb // LANES

    @pl.when(flag[0] == 0)
    def _():
        s = halves(s_ref[...])
        d = halves(d_ref[...])
        add = None
        for h in range(parts):
            flat = tops[h]
            top = jnp.concatenate([flat[pl.ds(q, piece, stride=per), :] for q in range(per)], axis=1)
            span = slice(h * piece, (h + 1) * piece)
            part = dot3((d[0][:, span], d[1][:, span]), halves(top), ((1,), (0,)))
            add = part if add is None else add + part
        for h in range(parts):
            span = slice(h * piece, (h + 1) * piece)
            out = dot3(s, halves(lows[h][...]), ((1,), (1,)))
            high_ref[:nb, span], low_ref[:nb, span] = halves(out[:nb])
            high_ref[nb:, span], low_ref[nb:, span] = halves(add[:, span] - out[nb:])

    @pl.when(flag[0] != 0)
    def _():
        high_ref[:nb], low_ref[:nb] = halves(-s_ref[:nb])
        high_ref[nb:], low_ref[nb:] = halves(s_ref[nb:])


def factors(flag, s, d, lows, tops):
    nb = d.shape[0]
    parts = len(lows)
    vmem = pl.BlockSpec(memory_space=pltpu.VMEM)
    return pl.pallas_call(
        functools.partial(factor_kernel, parts),
        out_shape=[jax.ShapeDtypeStruct((2 * nb, nb), BF16)] * 2,
        in_specs=[pl.BlockSpec(memory_space=pltpu.SMEM)] + [vmem] * (2 + 2 * parts),
        out_specs=[vmem] * 2,
        compiler_params=pltpu.CompilerParams(vmem_limit_bytes=40 << 20),
        cost_estimate=pl.CostEstimate(flops=18 * nb**3, bytes_accessed=24 * nb * nb, transcendentals=0),
        name="factors",
    )(flag, s, d, *lows, *tops)


def split_kernel(per, flags, panel_ref, high_ref, low_ref):
    tile = high_ref.shape[0]
    drop = jnp.logical_and(flags[0] != 0, pl.program_id(0) == 0)
    for q in range(per):
        value = jnp.where(drop, 0.0, panel_ref[pl.ds(q, tile, stride=per), :])
        span = slice(q * LANES, (q + 1) * LANES)
        high_ref[:, span], low_ref[:, span] = halves(value)


def split_panel(flags, panel, tile, per):
    rows = panel.shape[0] // per
    out = pl.BlockSpec((tile, per * LANES), lambda i: (i, 0))
    return pl.pallas_call(
        functools.partial(split_kernel, per),
        grid=(rows // tile,),
        out_shape=[jax.ShapeDtypeStruct((rows, per * LANES), BF16)] * 2,
        in_specs=[pl.BlockSpec(memory_space=pltpu.SMEM), pl.BlockSpec((tile * per, LANES), lambda i: (i, 0))],
        out_specs=[out] * 2,
        compiler_params=pltpu.CompilerParams(vmem_limit_bytes=40 << 20),
        cost_estimate=pl.CostEstimate(flops=0, bytes_accessed=8 * rows * per * LANES, transcendentals=0),
        name="split_panel",
    )(flags, panel)


def split_lower_kernel(flags, lower_ref, high_ref, low_ref):
    top = jnp.logical_and(flags[0] != 0, pl.program_id(0) == 0)
    shape = lower_ref.shape
    same = lax.broadcasted_iota(jnp.int32, shape, 0) == lax.broadcasted_iota(jnp.int32, shape, 1)
    value = jnp.where(top, jnp.where(same, -1.0, 0.0), lower_ref[...])
    high_ref[...], low_ref[...] = halves(value)


def split_lower(flags, lower, tile):
    spec = pl.BlockSpec((tile, lower.shape[1]), lambda i: (i, 0))
    return pl.pallas_call(
        split_lower_kernel,
        grid=(lower.shape[0] // tile,),
        out_shape=[jax.ShapeDtypeStruct(lower.shape, BF16)] * 2,
        in_specs=[pl.BlockSpec(memory_space=pltpu.SMEM), spec],
        out_specs=[spec] * 2,
        compiler_params=pltpu.CompilerParams(vmem_limit_bytes=40 << 20),
        cost_estimate=pl.CostEstimate(flops=0, bytes_accessed=8 * lower.size, transcendentals=0),
        name="split_lower",
    )(flags, lower)


def update_kernel(group, start, flags, a_ref, ph_ref, pl_ref, lh_ref, ll_ref, *refs):
    out_ref, token_ref = refs[-2:]
    token_ref[...] = jnp.zeros_like(token_ref)
    tile = a_ref.shape[0]
    chunks = a_ref.shape[1]
    depth = ph_ref.shape[1]
    per = refs[0].shape[1] // LANES
    a2 = a_ref.reshape(tile * chunks, LANES)
    o2 = out_ref.reshape(tile * chunks, LANES)
    top = jnp.logical_and(flags[0] != 0, pl.program_id(0) == -start)
    first = jnp.logical_and(flags[1] != 0, group == 0)
    mul = functools.partial(jnp.dot, preferred_element_type=F32)
    for pair in range(chunks // 2):
        block, at = divmod(2 * pair, per)
        yh_ref, yl_ref = refs[2 * block], refs[2 * block + 1]
        span = slice(at * LANES, (at + 2) * LANES)
        acc = mul(ph_ref[...], yh_ref[:depth, span])
        acc = acc + mul(pl_ref[...], yh_ref[:depth, span])
        acc = acc + mul(ph_ref[...], yl_ref[:depth, span])
        acc = acc + mul(lh_ref[...], yh_ref[depth:, span])
        acc = acc + mul(ll_ref[...], yh_ref[depth:, span])
        acc = acc + mul(lh_ref[...], yl_ref[depth:, span])
        drop = jnp.logical_or(top, first) if block == 0 else top
        for k in range(2):
            where = (pl.ds(2 * pair + k, tile, stride=chunks), slice(None))
            a = jnp.where(drop, 0.0, a2[where])
            o2[where] = a - acc[:, k * LANES : (k + 1) * LANES]


def update(group, start, steps, flags, a, xs, ys, previous, tile):
    rows, chunks, _ = a.shape
    depth = xs[0].shape[1]
    nb = ys[0].shape[1]
    mine = len(ys) // 2 * (nb // LANES)
    spec = pl.BlockSpec((tile, mine, LANES), lambda i: (i + start, group, 0))
    xspec = pl.BlockSpec((tile, depth), lambda i: (i + start, 0))
    yspec = pl.BlockSpec((2 * depth, nb), lambda i: (0, 0))
    operands = [flags, a, *xs, *ys]
    in_specs = [pl.BlockSpec(memory_space=pltpu.SMEM), spec] + [xspec] * len(xs) + [yspec] * len(ys)
    aliases = {}
    if previous is not None:
        aliases = {len(operands): 0}
        operands.append(previous)
        in_specs.append(pl.BlockSpec(memory_space=pl.ANY))
    done = steps * tile
    return pl.pallas_call(
        functools.partial(update_kernel, group, start),
        grid=(steps,),
        out_shape=[jax.ShapeDtypeStruct(a.shape, F32), jax.ShapeDtypeStruct((8, LANES), F32)],
        in_specs=in_specs,
        out_specs=[spec, pl.BlockSpec((8, LANES), lambda i: (0, 0))],
        input_output_aliases=aliases,
        compiler_params=pltpu.CompilerParams(vmem_limit_bytes=56 << 20),
        cost_estimate=pl.CostEstimate(
            flops=12 * done * mine * LANES * depth, bytes_accessed=8 * done * mine * LANES + 8 * done * depth,
            transcendentals=0,
        ),
        name="update",
    )(*operands)


def tie(sent, *waits):
    return list(lax.optimization_barrier((tuple(sent), waits))[0])


def arrived(got, k, distance, farthest, value):
    for d in range(1, farthest + 1):
        value = jnp.where(distance == d, got[k + d - 1], value)
    return value


def body(stiffness, lower_panel, diag_inverse):
    highest = lax.Precision.HIGHEST
    rows = lax.axis_size("row")
    cols = lax.axis_size("col")
    my_row = lax.axis_index("row")
    my_col = lax.axis_index("col")
    brows, _, nb, bcols, _, _ = stiffness.shape
    per = nb // LANES
    ratio = cols // rows
    split = 2
    piece = nb // split
    last = rows - 1
    home = my_col % rows
    col0 = my_col == 0
    flags = jnp.stack([my_row == 0, col0]).astype(jnp.int32)

    def dev(r, c):
        return r * cols + c

    def send(x, pairs):
        return lax.ppermute(x, ("row", "col"), pairs)

    a4 = stiffness.reshape(brows * nb, bcols, per, LANES)
    a = stiffness.reshape(brows * nb, bcols * per, LANES)
    lower = lower_panel[:, 0]

    top_own = [a4[s * piece : (s + 1) * piece, b].reshape(-1, LANES) for b in range(bcols) for s in range(split)]
    top_pairs = [(dev(r, c), dev(r + 1, c)) for r in range(last) for c in range(cols)]
    grouped = lower.reshape(bcols, ratio, nb, nb)
    mine = lax.dynamic_index_in_dim(grouped, my_col // rows, 1, keepdims=False)
    up_own = [mine[b, s * piece : (s + 1) * piece] for b in range(bcols) for s in range(split)]
    down_own = [mine[b] for b in range(bcols)]
    detour = {c: c ^ 2 for c in range(cols) if c % rows == 1} if (rows, cols) == (4, 8) else {}
    starts = {c: c % rows for c in range(cols) if c not in detour}
    starts.update({via: c % rows for c, via in detour.items()})
    up_pairs = [(dev(r, c), dev(r + 1, c)) for c, s in starts.items() for r in range(s, last)]
    up_source = my_row == home
    if detour:
        up_source = jnp.where(home == 3, my_row == 1, up_source)
    down_pairs = [(dev(r, c), dev(r - 1, c)) for c in range(cols) for r in range(c % rows, 0, -1)]
    side_pairs = [(dev(r, via), dev(r, c)) for c, via in detour.items() for r in range(2, rows)]

    panel = a4[:, 0].reshape(-1, LANES)
    share = panel.shape[0] // cols

    def nxt(own, got, source):
        t = len(got)
        if t == 0:
            return own[0]
        return jnp.where(source, own[t], got[-1]) if t < len(own) else got[-1]

    def top_at(k):
        return arrived(top_got, k, my_row, last, top_own[k])

    def low_at(k):
        value = arrived(up_got, k, my_row - home, last, up_own[k])
        down_k = [g[(k % split) * piece : (k % split + 1) * piece] for g in down_got]
        value = arrived(down_k, k // split, home - my_row, last, value)
        for r in range(2, rows) if detour else ():
            here = jnp.logical_and(home == 1, my_row == r)
            value = jnp.where(here, side_got[k + r - 2], value)
        return value

    def factors_of(b, d=diag_inverse):
        special = jnp.logical_and(col0, b == 0).astype(jnp.int32).reshape(1)
        here = range(b * split, (b + 1) * split)
        return factors(special, s, d, [low_at(k) for k in here], [top_at(k) for k in here])

    def spread(x, bit):
        span = 1 << bit
        pairs = [(dev(r, c), dev(r, c + span)) for r in range(rows) for c in range(0, cols, 2 * span)]
        return jnp.where(my_col % (2 * span) == span, send(x, pairs), x)

    def scales():
        c_block = jnp.dot(diag_inverse, corner.reshape(nb, nb), precision=highest)
        c_block = jnp.dot(c_block, diag_inverse.T, precision=highest)
        return jnp.concatenate([diag_inverse.T, c_block])

    count = bcols * split
    top_steps = count + last - 1
    down_steps = bcols + last - 1
    corner_at = split + last - 1
    bits = cols.bit_length() - 1
    ready = 2 * split + last - 1
    parts = max(top_steps - ready - 1, 1)
    early = bcols > 2 and corner_at + bits <= ready + 1 and top_steps - ready > 1
    bit = bits
    bounds = [brows * k // parts for k in range(parts + 1)]
    top_got, up_got, down_got, side_got = [], [], [], []
    corner = panel_all = out = s = None
    ys, waits = {}, []
    for t in range(top_steps):
        sent = [nxt(top_own, top_got, my_row == 0)]
        if t == corner_at:
            corner = jnp.concatenate([top_at(k) for k in range(split)])
        hop = t >= corner_at and bit > 0
        if hop:
            bit -= 1
            sent.append(corner)
        if t:
            tied = [top_got[-1], *waits]
            tied += up_got[t - 1 :] if t >= ready else up_got[t - 2 : t - 1]
            sent = tie(sent, *tied)
        top_got.append(send(sent[0], top_pairs))
        if hop:
            corner = spread(sent[1], bit)
        sent = [nxt(up_own, up_got, up_source)]
        if detour and t:
            sent.append(up_got[t - 1])
        go_down = len(down_got) < down_steps and t >= (4 * len(down_got) + 1) // 3
        if go_down:
            sent.append(nxt(down_own, down_got, my_row == home))
        if t:
            late = down_got[max(len(down_got) - 2, 0) : len(down_got) - 1] + side_got[max(t - 3, 0) : t - 2]
            sent = tie(sent, up_got[-1], top_got[t - 1], *late, *waits)
        up_got.append(send(sent[0], up_pairs))
        if detour and t:
            side_got.append(send(sent[1], side_pairs))
        if go_down:
            down_got.append(send(sent[-1], down_pairs))
        waits = []
        if t == 0:
            deals = [panel[c * share : (c + 1) * share] for c in range(cols)]
            mine_share, *deals = tie(deals, top_got[0])
            dealt = [send(x, [(dev(r, 0), dev(r, c + 1)) for r in range(rows)]) for c, x in enumerate(deals)]
        if t == 1:
            right = split_lower(flags, lower.reshape(brows * nb, nb), nb)
            waits = [right[0]]
        if t == min(3, top_steps - 1):
            share_got = jnp.where(col0, mine_share, functools.reduce(jnp.add, tie(dealt, top_got[t], up_got[t])))
            panel_all = lax.all_gather(share_got, "col", axis=0, tiled=True)
        if early and t == ready:
            s = scales()
            (own_flags,) = tie([flags], top_got[t - 1])
            xs = [*split_panel(own_flags, panel_all, nb, per), *right]
            ys[0] = [*factors_of(0)]
            waits = [xs[0], ys[0][0]]
        if early and t > ready:
            k = t - ready - 1
            own_flags, d = tie([flags, diag_inverse], top_got[t - 1], up_got[t - 1])
            if k == 0:
                ys[0] += factors_of(1, d)
            out, token = update(
                0, bounds[k], bounds[k + 1] - bounds[k], own_flags, a, xs, ys[0], out, nb
            )
            waits = [token]
            if t == top_steps - 1:
                ys[1] = [*factors_of(2, d)]
    if detour:
        side_got.append(send(up_got[-1], side_pairs))
    while len(down_got) < down_steps:
        down_got.append(send(nxt(down_own, down_got, my_row == home), down_pairs))
    if not early:
        while bit > 0:
            bit -= 1
            corner = spread(corner, bit)
        s = scales()
        xs = [*split_panel(flags, panel_all, nb, per), *right]
    for group in range(int(early), bcols // 2):
        done = ys.get(group) or factors_of(2 * group)
        ys[group] = [*done, *factors_of(2 * group + 1)]
        out, _ = update(group, 0, brows, flags, a, xs, ys[group], out, nb)
    return out.reshape(stiffness.shape)


def solution(mesh):
    in_specs = (P(None, "row", None, None, "col", None), P(None, "row", None, None), P())
    out_specs = P(None, "row", None, None, "col", None)
    return jax.shard_map(body, mesh=mesh, in_specs=in_specs, out_specs=out_specs, check_vma=False)
```
